512 devices in a mesh: seq: 512 (over x, z, y, core).
Axes of the slice: x: 4, y: 8, z: 8, core: 2. Of those that a mesh axis runs over, the one named last changes fastest.
Arguments:
- queries: bfloat16 [196608, 1024], P('seq')
- keys: bfloat16 [196608, 256], P('seq')
- values: bfloat16 [196608, 256], P('seq'), may hold values from -6 to 6
- out_weight: bfloat16 [1024, 2048], replicated, may hold values from -9 to 9
Outputs:
- projected: bfloat16 [196608, 2048], P('seq')
The draws below stay inside these ranges and needn't reach their ends.
All inputs are finite; a program needn't handle non-finite values.
Results may differ from the reference program's by a relative error of at most 0.0057.
Values may be sent and summed in bfloat16 or wider, within the bound.
No kernel may reach another device: no remote copies, remote signals or barrier semaphores. Data moves between devices by JAX's collectives and lax.ppermute only.
A program may use at most 64 MiB of HBM per device.

```python
import jax
import jax.numpy as jnp
from jax import lax

D = 2048
QH = 8
KVH = 2
HD = 128
TOK_DEV = 384
WINDOW = 192
TOKENS = 196608
N_SEQ = 512


def shared_keys(key):
    return jnp.clip(jax.random.normal(key, (TOKENS, KVH * HD), jnp.float32), -6.0, 6.0)


def marked_at(position):
    return (position % 61 == 7) & (position >= 16 * TOK_DEV) & (position < TOKENS)


def pair_of(position):
    return position // 61 % 5


def first_offsets():
    return jnp.array([2 * TOK_DEV, WINDOW // 2, 8 * TOK_DEV, 16 * TOK_DEV, 4 * TOK_DEV], jnp.int32)


def second_offsets():
    return jnp.array([8 * TOK_DEV, 16 * TOK_DEV, 4 * TOK_DEV, WINDOW // 2, 2 * TOK_DEV], jnp.int32)


def draw_keys(key, part):
    base = shared_keys(key)
    position = jnp.arange(TOKENS, dtype=jnp.int32)
    first = first_offsets()
    second = second_offsets()
    mixed = base
    for which in range(5):
        owner = position + second[which]
        live = marked_at(owner) & (pair_of(owner) == which)
        source = jnp.clip(owner - first[which], 0, TOKENS - 1).astype(jnp.int32)
        copied = jnp.take(base, source, axis=0)
        mixed = jnp.where(live[:, None], 0.99 * copied, mixed)
    return mixed.astype(jnp.bfloat16)


def draw_queries(key, part):
    key = jax.random.fold_in(key, 23)
    drawn = jax.random.normal(key, (TOKENS, QH * HD), jnp.float32)
    return drawn.astype(jnp.bfloat16)


def steps_of(key, extent, split, least, high):
    loudness = 1.0
    for dim, shards_of in split:
        draws = jax.random.uniform(jax.random.fold_in(jax.random.fold_in(key, 6), dim), (shards_of,), jnp.float32, least / len(split), high / len(split))
        loudness = loudness * jnp.repeat(jnp.exp(draws), extent[dim] // shards_of).reshape((-1,) + (1,) * (len(extent) - 1 - dim))
    return loudness


def normal_values(key, shape, spread, limit, pieces=(), kind=jnp.bfloat16):
    result = jax.random.normal(key, shape, jnp.float32) * spread
    if len(pieces) > 0:
        result = steps_of(key, shape, pieces, -0.22, 0.18) * result
    return jnp.clip(result, min=-limit, max=limit).astype(kind)


def setup_inputs(seed: int = 0) -> dict:
    key_of = jax.random.split(jax.random.key(seed), 5)
    queries = draw_queries(jax.random.fold_in(key_of[4], 71), 0)
    keys = draw_keys(jax.random.fold_in(key_of[4], 71), 0)
    values = normal_values(key_of[2], (TOKENS, KVH * HD), 1.0, 6.0, ((0, 512),))
    out_weight = normal_values(key_of[3], (QH * HD, D), 1.5, 9.0)
    return {"queries": queries, "keys": keys, "values": values, "out_weight": out_weight}


def reference(queries, keys, values, out_weight):
    group = QH // KVH
    span = WINDOW + 5 * TOK_DEV
    scale = 1.0 / (HD ** 0.5)
    blank = jnp.zeros((WINDOW, KVH * HD), jnp.bfloat16)
    keys_pad = jnp.concatenate([blank, keys], axis=0)
    values_pad = jnp.concatenate([blank, values], axis=0)
    rows = jnp.arange(TOK_DEV, dtype=jnp.int32)[:, None]
    offset = jnp.arange(WINDOW + TOK_DEV, dtype=jnp.int32)[None, :] - WINDOW

    def one_block(block):
        start = (block * TOK_DEV).astype(jnp.int32)
        query_rows = lax.dynamic_slice_in_dim(queries, start, TOK_DEV, 0)
        key_parts = [lax.dynamic_slice_in_dim(keys_pad, start, WINDOW + TOK_DEV, 0)]
        value_parts = [lax.dynamic_slice_in_dim(values_pad, start, WINDOW + TOK_DEV, 0)]
        near = (offset <= rows) & (offset >= rows - WINDOW) & ((offset >= 0) | (block >= 1))
        mask_parts = [near]
        for distance in (2, 4, 8, 16):
            source = (jnp.maximum(block - distance, 0) * TOK_DEV).astype(jnp.int32)
            key_parts.append(lax.dynamic_slice_in_dim(keys, source, TOK_DEV, 0))
            value_parts.append(lax.dynamic_slice_in_dim(values, source, TOK_DEV, 0))
            mask_parts.append(jnp.broadcast_to(block >= distance, (TOK_DEV, TOK_DEV)))
        key_all = jnp.concatenate(key_parts, axis=0).reshape(span, KVH, HD).astype(jnp.float32)
        value_all = jnp.concatenate(value_parts, axis=0).reshape(span, KVH, HD).astype(jnp.float32)
        allowed = jnp.concatenate(mask_parts, axis=1)
        query_four = query_rows.reshape(TOK_DEV, KVH, group, HD).astype(jnp.float32)
        scores = jnp.einsum('tgjd,lgd->gjtl', query_four, key_all) * scale
        scores = jnp.where(allowed, scores, -1e30)
        top = jnp.max(scores, axis=-1, keepdims=True)
        weights = jnp.where(allowed, jnp.exp(scores - top), 0.0)
        totals = jnp.sum(weights, axis=-1, keepdims=True)
        rounded = lax.optimization_barrier(weights.astype(jnp.bfloat16)).astype(jnp.float32)
        summed = jnp.einsum('gjtl,lgd->tgjd', rounded, value_all)
        attended = (summed / jnp.transpose(totals, (2, 0, 1, 3))).reshape(TOK_DEV, QH * HD).astype(jnp.bfloat16)
        return jnp.dot(attended, out_weight, preferred_element_type=jnp.float32).astype(jnp.bfloat16)

    blocks = lax.map(one_block, jnp.arange(N_SEQ, dtype=jnp.int32))
    return blocks.reshape(TOKENS, D)
```

```python
import functools
import math

import jax
import jax.numpy as jnp
from jax import lax
from jax.experimental import pallas as pl
from jax.experimental.pallas import tpu as pltpu
from jax.sharding import PartitionSpec as P

HEAD = 128
STRIP = 128
FAR = (2, 4, 8, 16)
LOW = -1e30
SCALE = math.log2(math.e) / math.sqrt(HEAD)
LIMIT = 40 * 1024 * 1024
VMEM = pl.BlockSpec(memory_space=pltpu.VMEM)
ANY = pl.BlockSpec(memory_space=pl.ANY)


def shifted(block, distance):
    devices = lax.axis_size("seq")
    return lax.ppermute(block, "seq", [(i, (i + distance) % devices) for i in range(devices)])


def pack_kernel(keys, values, both, tail):
    rows, width = keys.shape
    reach = rows - tail.shape[0]
    both[:, :width] = keys[...]
    both[:, width:] = values[...]
    tail[:, :width] = keys[reach:]
    tail[:, width:] = values[reach:]


def pack(keys, values):
    rows, width = keys.shape
    return pl.pallas_call(
        pack_kernel,
        out_shape=(
            jax.ShapeDtypeStruct((rows, 2 * width), keys.dtype),
            jax.ShapeDtypeStruct((rows // 2, 2 * width), keys.dtype),
        ),
        in_specs=[VMEM] * 2,
        out_specs=(VMEM, VMEM),
        name="pack",
    )(keys, values)


def tiles_of(rows, kv_heads):
    return [(g, j) for g in range(kv_heads) for j in range(rows // STRIP)]


def query_tile(queries, g, j, group):
    rows = slice(j * STRIP, (j + 1) * STRIP)
    return jnp.concatenate(
        [queries[rows, (g * group + h) * HEAD : (g * group + h + 1) * HEAD] for h in range(group)],
        axis=0,
    )


def scores_of(key_rows, query):
    return lax.dot_general(
        key_rows, query, (((1,), (1,)), ((), ())), preferred_element_type=jnp.float32
    )


def summed_of(value_rows, weights):
    return lax.dot_general(
        value_rows,
        weights.astype(jnp.bfloat16),
        (((0,), (0,)), ((), ())),
        preferred_element_type=jnp.float32,
    )


def near_kernel(queries, both, tail, acc, stats, joined):
    rows, width = queries.shape
    kv_width = both.shape[1] // 2
    kv_heads = kv_width // HEAD
    group = width // HEAD // kv_heads
    reach = tail.shape[0]
    me = lax.axis_index("seq")
    joined[:reach] = tail[...]
    joined[reach:] = both[...]
    span = reach + STRIP
    columns = group * STRIP
    key_at = lax.broadcasted_iota(jnp.int32, (span, columns), 0)
    row_at = lax.broadcasted_iota(jnp.int32, (1, columns), 1) % STRIP
    for t, (g, j) in enumerate(tiles_of(rows, kv_heads)):
        first = j * STRIP
        key_rows = joined[first : first + span, g * HEAD : (g + 1) * HEAD]
        value_rows = joined[first : first + span, kv_width + g * HEAD : kv_width + (g + 1) * HEAD]
        scores = scores_of(key_rows, query_tile(queries, g, j, group))
        least = jnp.where(me >= 1, 0, max(reach - first, 0))
        allowed = (key_at >= jnp.maximum(row_at, least)) & (key_at <= row_at + reach)
        scores = jnp.where(allowed, scores, LOW)
        top = jnp.max(scores, axis=0, keepdims=True)
        weights = jnp.exp2(scores * SCALE - top * SCALE)
        stats[t : t + 1] = top
        stats[8 + t : 9 + t] = jnp.sum(weights, axis=0, keepdims=True)
        acc[t] = summed_of(value_rows, weights)


def far_step(queries, parts, top, total, acc, g, j, kv_width, group, me):
    query = query_tile(queries, g, j, group)
    scores = []
    for ref, distance in parts:
        part = scores_of(ref[:, g * HEAD : (g + 1) * HEAD], query)
        if me is not None:
            part = jnp.where(me >= distance, part, LOW)
        scores.append(part)
    new_top = top
    for part in scores:
        new_top = jnp.maximum(new_top, jnp.max(part, axis=0, keepdims=True))
    fade = jnp.exp2((top - new_top) * SCALE)
    total = total * fade
    acc = acc * fade
    for part, (ref, _) in zip(scores, parts):
        weights = jnp.exp2(part * SCALE - new_top * SCALE)
        total = total + jnp.sum(weights, axis=0, keepdims=True)
        value_rows = ref[:, kv_width + g * HEAD : kv_width + (g + 1) * HEAD]
        acc = acc + summed_of(value_rows, weights)
    return new_top, total, acc


def with_or_without_mask(distances, body):
    me = lax.axis_index("seq")
    far = max(distances)

    @pl.when(me >= far)
    def _():
        body(None)

    @pl.when(me < far)
    def _():
        body(me)


def far_kernel(distances, queries, acc_in, stats_in, *refs):
    parts = list(zip(refs[: len(distances)], distances))
    acc, stats = refs[len(distances) :]
    rows, width = queries.shape
    kv_width = parts[0][0].shape[1] // 2
    kv_heads = kv_width // HEAD
    group = width // HEAD // kv_heads

    def body(me):
        for t, (g, j) in enumerate(tiles_of(rows, kv_heads)):
            top, total, summed = far_step(
                queries, parts, stats_in[t : t + 1], stats_in[8 + t : 9 + t], acc_in[t],
                g, j, kv_width, group, me,
            )
            stats[t : t + 1] = top
            stats[8 + t : 9 + t] = total
            acc[t] = summed

    with_or_without_mask(distances, body)


def last_kernel(distances, queries, acc_in, stats_in, *refs):
    parts = list(zip(refs[: len(distances)], distances))
    weight_hbm, out_hbm, weight, attended, staged, in_sems, out_sems = refs[len(distances) :]
    rows, width = queries.shape
    kv_width = parts[0][0].shape[1] // 2
    kv_heads = kv_width // HEAD
    group = width // HEAD // kv_heads
    pieces, _, piece = staged.shape

    def fetch(n):
        columns = pl.ds(n * piece, piece)
        return pltpu.make_async_copy(weight_hbm.at[:, columns], weight.at[:, columns], in_sems.at[n])

    def put(n):
        return pltpu.make_async_copy(staged.at[n], out_hbm.at[:, pl.ds(n * piece, piece)], out_sems.at[n])

    for n in range(pieces):
        fetch(n).start()

    def body(me):
        for t, (g, j) in enumerate(tiles_of(rows, kv_heads)):
            _, total, summed = far_step(
                queries, parts, stats_in[t : t + 1], stats_in[8 + t : 9 + t], acc_in[t],
                g, j, kv_width, group, me,
            )
            done = (summed / total).astype(jnp.bfloat16)
            for h in range(group):
                head = g * group + h
                attended[j * STRIP : (j + 1) * STRIP, head * HEAD : (head + 1) * HEAD] = done[
                    :, h * STRIP : (h + 1) * STRIP
                ].T

    with_or_without_mask(distances, body)
    for n in range(pieces):
        fetch(n).wait()
        staged[n] = jnp.dot(
            attended[...], weight[:, n * piece : (n + 1) * piece], preferred_element_type=jnp.float32
        ).astype(jnp.bfloat16)
        put(n).start()
    for n in range(pieces):
        put(n).wait()


def cost(rows, keys, width, extra=0):
    return pl.CostEstimate(
        flops=4 * rows * keys * width + extra,
        bytes_accessed=4 * rows * width * 2 + 4 * keys * 512,
        transcendentals=rows * keys * width // HEAD,
    )


def near(queries, both, tail):
    rows, width = queries.shape
    strips = rows // STRIP
    kv_heads = both.shape[1] // 2 // HEAD
    columns = width // HEAD // kv_heads * STRIP
    return pl.pallas_call(
        near_kernel,
        out_shape=(
            jax.ShapeDtypeStruct((kv_heads * strips, HEAD, columns), jnp.float32),
            jax.ShapeDtypeStruct((16, columns), jnp.float32),
        ),
        in_specs=[VMEM] * 3,
        out_specs=(VMEM, VMEM),
        scratch_shapes=[pltpu.VMEM((rows + tail.shape[0], both.shape[1]), both.dtype)],
        compiler_params=pltpu.CompilerParams(vmem_limit_bytes=LIMIT),
        cost_estimate=cost(rows, 320, width),
        name="near",
    )(queries, both, tail)


def far(queries, state, blocks, distances):
    rows, width = queries.shape
    acc, stats = state
    return pl.pallas_call(
        functools.partial(far_kernel, distances),
        out_shape=tuple(jax.ShapeDtypeStruct(x.shape, x.dtype) for x in state),
        in_specs=[VMEM] * (3 + len(blocks)),
        out_specs=(VMEM, VMEM),
        compiler_params=pltpu.CompilerParams(vmem_limit_bytes=LIMIT),
        cost_estimate=cost(rows, sum(b.shape[0] for b in blocks), width),
        name="far",
    )(queries, acc, stats, *blocks)


def last(queries, state, blocks, distances, out_weight):
    rows, width = queries.shape
    wide = out_weight.shape[1]
    piece = 512
    acc, stats = state
    return pl.pallas_call(
        functools.partial(last_kernel, distances),
        out_shape=jax.ShapeDtypeStruct((rows, wide), jnp.bfloat16),
        in_specs=[VMEM] * (3 + len(blocks)) + [ANY],
        out_specs=ANY,
        scratch_shapes=[
            pltpu.VMEM(out_weight.shape, jnp.bfloat16),
            pltpu.VMEM((rows, width), jnp.bfloat16),
            pltpu.VMEM((wide // piece, rows, piece), jnp.bfloat16),
            pltpu.SemaphoreType.DMA((wide // piece,)),
            pltpu.SemaphoreType.DMA((wide // piece,)),
        ],
        compiler_params=pltpu.CompilerParams(vmem_limit_bytes=LIMIT),
        cost_estimate=cost(rows, sum(b.shape[0] for b in blocks), width, 2 * rows * width * wide),
        name="last",
    )(queries, acc, stats, *blocks, out_weight)


def on_device(queries, keys, values, out_weight):
    both, tail = pack(keys, values)
    before = shifted(tail, 1)
    behind = shifted(both, 2)
    later = shifted(both, 16)
    eighth = shifted(both, 8)
    fourth = shifted(behind, 2)
    state = near(queries, both, before)
    state = far(queries, state, (behind, later), (2, 16))
    state = far(queries, state, (fourth,), (4,))
    return last(queries, state, (eighth,), (8,), out_weight)


def solution(mesh):
    in_specs = (P("seq", None), P("seq", None), P("seq", None), P())
    return jax.shard_map(
        on_device, mesh=mesh, in_specs=in_specs, out_specs=P("seq", None), check_vma=False
    )
```

```python
import functools
import math

import jax
import jax.numpy as jnp
from jax import lax
from jax.experimental import pallas as pl
from jax.experimental.pallas import tpu as pltpu
from jax.sharding import PartitionSpec as P

HEAD = 128
STRIP = 128
RING = 8
LOW = -1e30
MOST = 2.0**80
SCALE = math.log2(math.e) / math.sqrt(HEAD)
LIMIT = 36 * 1024 * 1024
VMEM = pl.BlockSpec(memory_space=pltpu.VMEM)
ANY = pl.BlockSpec(memory_space=pl.ANY)


def shifted(block, distance):
    devices = lax.axis_size("seq")
    return lax.ppermute(block, "seq", [(i, (i + distance) % devices) for i in range(devices)])


def routed(block, target):
    chips = lax.axis_size("seq") // 2
    routes = [(2 * c + k, 2 * (target(c) % chips) + k) for c in range(chips) for k in range(2)]
    return lax.ppermute(block, "seq", routes)


def back(c, hops):
    return c - hops if c % RING >= hops else c - hops + RING


def from_back(c, hops):
    return (c + hops if c % RING + hops < RING else c + hops - RING) + 4


def pack_kernel(keys, values, both, tail, *rest):
    *halves, sems = rest
    rows, width = keys.shape
    copies = [
        pltpu.make_async_copy(source, both.at[:, pl.ds(n * width, width)], sems.at[n])
        for n, source in enumerate((keys, values))
    ]
    for copy in copies:
        copy.start()
    for copy in copies:
        copy.wait()
    tail[...] = both[rows - tail.shape[0] :]
    first = 0
    for half in halves:
        half[...] = both[first : first + half.shape[0]]
        first += half.shape[0]


def pack(keys, values, split=None):
    rows, width = keys.shape
    counts = [rows, rows // 2] + ([split, rows - split] if split else [])
    return pl.pallas_call(
        pack_kernel,
        out_shape=tuple(jax.ShapeDtypeStruct((n, 2 * width), keys.dtype) for n in counts),
        in_specs=[pl.BlockSpec(memory_space=pltpu.HBM)] * 2,
        out_specs=(VMEM,) * len(counts),
        scratch_shapes=[pltpu.SemaphoreType.DMA((2,))],
        compiler_params=pltpu.CompilerParams(vmem_limit_bytes=8 * 1024 * 1024),
        name="pack",
    )(keys, values)


def tiles_of(rows, kv_heads):
    return [(g, j) for g in range(kv_heads) for j in range(rows // STRIP)]


def query_tile(queries, g, j, group):
    rows = slice(j * STRIP, (j + 1) * STRIP)
    return jnp.concatenate(
        [queries[rows, (g * group + h) * HEAD : (g * group + h + 1) * HEAD] for h in range(group)],
        axis=0,
    )


def scores_of(key_rows, query):
    return lax.dot_general(
        key_rows, query, (((1,), (1,)), ((), ())), preferred_element_type=jnp.float32
    )


def summed_of(value_rows, weights):
    return lax.dot_general(
        value_rows,
        weights.astype(jnp.bfloat16),
        (((0,), (0,)), ((), ())),
        preferred_element_type=jnp.float32,
    )


def sizes_of(queries, kv_width):
    width = queries.shape[1]
    kv_heads = kv_width // HEAD
    return kv_heads, width // HEAD // kv_heads


def in_turn(tiles, ahead, finish):
    scores = ahead(0, *tiles[0])
    for t, (g, j) in enumerate(tiles):
        later = ahead(t + 1, *tiles[t + 1]) if t + 1 < len(tiles) else None
        finish(t, g, j, scores)
        scores = later


def near_kernel(queries, both, tail, acc, stats, joined):
    rows = queries.shape[0]
    kv_width = both.shape[1] // 2
    kv_heads, group = sizes_of(queries, kv_width)
    reach = tail.shape[0]
    me = lax.axis_index("seq")
    joined[:reach] = tail[...]
    joined[reach:] = both[...]
    span = reach + STRIP
    columns = group * STRIP
    key_at = lax.broadcasted_iota(jnp.int32, (span, columns), 0)
    row_at = lax.broadcasted_iota(jnp.int32, (1, columns), 1) % STRIP

    def ahead(t, g, j):
        key_rows = joined[j * STRIP : j * STRIP + span, g * HEAD : (g + 1) * HEAD]
        return scores_of(key_rows, query_tile(queries, g, j, group))

    def finish(t, g, j, scores):
        first = j * STRIP
        value_rows = joined[first : first + span, kv_width + g * HEAD : kv_width + (g + 1) * HEAD]
        least = jnp.where(me >= 1, 0, max(reach - first, 0))
        allowed = (key_at >= jnp.maximum(row_at, least)) & (key_at <= row_at + reach)
        scores = jnp.where(allowed, scores, LOW)
        top = jnp.max(scores, axis=0, keepdims=True)
        weights = jnp.exp2(scores * SCALE - top * SCALE)
        stats[t : t + 1] = top
        stats[8 + t : 9 + t] = jnp.sum(weights, axis=0, keepdims=True)
        acc[t] = summed_of(value_rows, weights)

    in_turn(tiles_of(rows, kv_heads), ahead, finish)


def add_parts(queries, pieces, acc_in, stats_in, acc, stats, flag):
    rows = queries.shape[0]
    kv_width = pieces[0][0].shape[1] // 2
    kv_heads, group = sizes_of(queries, kv_width)
    tiles = tiles_of(rows, kv_heads)
    me = lax.axis_index("seq")
    flag[0] = 0

    def scores_with(parts, g, j):
        query = query_tile(queries, g, j, group)
        return [scores_of(ref[:, g * HEAD : (g + 1) * HEAD], query) for ref, _ in parts]

    def values_of(ref, g):
        return ref[:, kv_width + g * HEAD : kv_width + (g + 1) * HEAD]

    def same_top(parts):
        largest = []

        def finish(t, g, j, scores):
            top = stats_in[t : t + 1]
            total = stats_in[8 + t : 9 + t]
            summed = acc_in[t]
            for part, (ref, _) in zip(scores, parts):
                weights = jnp.exp2(part * SCALE - top * SCALE)
                total = total + jnp.sum(weights, axis=0, keepdims=True)
                summed = summed + summed_of(values_of(ref, g), weights)
            stats[t : t + 1] = top
            stats[8 + t : 9 + t] = total
            acc[t] = summed
            largest.append(total)

        in_turn(tiles, lambda t, g, j: scores_with(parts, g, j), finish)
        most = jnp.max(functools.reduce(jnp.maximum, largest))
        flag[0] = jnp.where(most < MOST, 0, 1)

    def new_top():
        def one(t, g, j):
            scores = [
                jnp.where(me >= distance, part, LOW)
                for part, (_, distance) in zip(scores_with(pieces, g, j), pieces)
            ]
            old = stats_in[t : t + 1]
            top = old
            for part in scores:
                top = jnp.maximum(top, jnp.max(part, axis=0, keepdims=True))
            fade = jnp.exp2(old * SCALE - top * SCALE)
            total = stats_in[8 + t : 9 + t] * fade
            summed = acc_in[t] * fade
            for part, (ref, _) in zip(scores, pieces):
                weights = jnp.exp2(part * SCALE - top * SCALE)
                total = total + jnp.sum(weights, axis=0, keepdims=True)
                summed = summed + summed_of(values_of(ref, g), weights)
            stats[t : t + 1] = top
            stats[8 + t : 9 + t] = total
            acc[t] = summed

        for t, (g, j) in enumerate(tiles):
            one(t, g, j)

    bounds = sorted({distance for _, distance in pieces})

    @pl.when(me < bounds[0])
    def _():
        acc[...] = acc_in[...]
        stats[...] = stats_in[...]

    for low, high in zip(bounds, bounds[1:] + [None]):
        here = me >= low if high is None else (me >= low) & (me < high)

        @pl.when(here)
        def _(low=low):
            same_top([(ref, distance) for ref, distance in pieces if distance <= low])

    @pl.when(flag[0] == 1)
    def _():
        new_top()


def far_kernel(distances, queries, acc_in, stats_in, *refs):
    pieces = list(zip(refs[: len(distances)], distances))
    acc, stats, flag = refs[len(distances) :]
    add_parts(queries, pieces, acc_in, stats_in, acc, stats, flag)


def last_kernel(distances, queries, acc_in, stats_in, *refs):
    pieces = list(zip(refs[: len(distances)], distances))
    weight, out_hbm, acc, stats, flag, attended, staged, sems = refs[len(distances) :]
    rows = queries.shape[0]
    kv_heads, group = sizes_of(queries, pieces[0][0].shape[1] // 2)
    cuts, _, cut = staged.shape
    add_parts(queries, pieces, acc_in, stats_in, acc, stats, flag)
    for t, (g, j) in enumerate(tiles_of(rows, kv_heads)):
        done = (acc[t] / stats[8 + t : 9 + t]).astype(jnp.bfloat16)
        for h in range(group):
            head = g * group + h
            attended[j * STRIP : (j + 1) * STRIP, head * HEAD : (head + 1) * HEAD] = done[
                :, h * STRIP : (h + 1) * STRIP
            ].T

    def put(n):
        return pltpu.make_async_copy(staged.at[n], out_hbm.at[:, pl.ds(n * cut, cut)], sems.at[n])

    for n in range(cuts):
        staged[n] = jnp.dot(
            attended[...], weight[:, n * cut : (n + 1) * cut], preferred_element_type=jnp.float32
        ).astype(jnp.bfloat16)
        put(n).start()
    for n in range(cuts):
        put(n).wait()


def cost(rows, keys, width, extra=0):
    return pl.CostEstimate(
        flops=4 * rows * keys * width + extra,
        bytes_accessed=4 * rows * width * 2 + 4 * keys * 512,
        transcendentals=rows * keys * width // HEAD,
    )


def near(queries, both, tail):
    rows, width = queries.shape
    strips = rows // STRIP
    kv_heads = both.shape[1] // 2 // HEAD
    columns = width // HEAD // kv_heads * STRIP
    return pl.pallas_call(
        near_kernel,
        out_shape=(
            jax.ShapeDtypeStruct((kv_heads * strips, HEAD, columns), jnp.float32),
            jax.ShapeDtypeStruct((16, columns), jnp.float32),
        ),
        in_specs=[VMEM] * 3,
        out_specs=(VMEM, VMEM),
        scratch_shapes=[pltpu.VMEM((rows + tail.shape[0], both.shape[1]), both.dtype)],
        compiler_params=pltpu.CompilerParams(vmem_limit_bytes=LIMIT),
        cost_estimate=cost(rows, 320, width),
        name="near",
    )(queries, both, tail)


def far(queries, state, blocks, distances):
    rows, width = queries.shape
    acc, stats = state
    return pl.pallas_call(
        functools.partial(far_kernel, distances),
        out_shape=tuple(jax.ShapeDtypeStruct(x.shape, x.dtype) for x in state),
        in_specs=[VMEM] * (3 + len(blocks)),
        out_specs=(VMEM, VMEM),
        scratch_shapes=[pltpu.SMEM((1,), jnp.int32)],
        compiler_params=pltpu.CompilerParams(vmem_limit_bytes=LIMIT),
        cost_estimate=cost(rows, sum(b.shape[0] for b in blocks), width),
        name="far",
    )(queries, acc, stats, *blocks)


def last(queries, state, blocks, distances, out_weight):
    rows, width = queries.shape
    wide = out_weight.shape[1]
    cut = 512
    acc, stats = state
    return pl.pallas_call(
        functools.partial(last_kernel, distances),
        out_shape=jax.ShapeDtypeStruct((rows, wide), jnp.bfloat16),
        in_specs=[VMEM] * (4 + len(blocks)),
        out_specs=ANY,
        scratch_shapes=[
            pltpu.VMEM(acc.shape, acc.dtype),
            pltpu.VMEM(stats.shape, stats.dtype),
            pltpu.SMEM((1,), jnp.int32),
            pltpu.VMEM((rows, width), jnp.bfloat16),
            pltpu.VMEM((wide // cut, rows, cut), jnp.bfloat16),
            pltpu.SemaphoreType.DMA((wide // cut,)),
        ],
        compiler_params=pltpu.CompilerParams(vmem_limit_bytes=LIMIT),
        cost_estimate=cost(rows, sum(b.shape[0] for b in blocks), width, 2 * rows * width * wide),
        name="last",
    )(queries, acc, stats, *blocks, out_weight)


def on_device(queries, keys, values, out_weight):
    both, tail, part, rest = pack(keys, values, 192)
    behind = shifted(both, 2)
    part = routed(part, lambda c: back(c, 1))
    before = shifted(tail, 1)
    eighth_rest = shifted(rest, 8)
    later = shifted(both, 16)
    behind, before, part = lax.optimization_barrier((behind, before, part))
    fourth = shifted(behind, 2)
    eighth_first = routed(part, lambda c: from_back(c, 1))
    state = near(queries, both, before)
    state = far(queries, state, (eighth_rest, later), (8, 16))
    state = far(queries, state, (behind, fourth), (2, 4))
    return last(queries, state, (eighth_first,), (8,), out_weight)


def solution(mesh):
    in_specs = (P("seq", None), P("seq", None), P("seq", None), P())
    return jax.shard_map(
        on_device, mesh=mesh, in_specs=in_specs, out_specs=P("seq", None), check_vma=False
    )
```

```python
import functools
import math

import jax
import jax.numpy as jnp
from jax import lax
from jax.experimental import pallas as pl
from jax.experimental.pallas import tpu as pltpu
from jax.sharding import PartitionSpec as P

HEAD = 128
STRIP = 128
RING = 8
LOW = -1e30
MOST = 2.0**80
SCALE = math.log2(math.e) / math.sqrt(HEAD)
LIMIT = 36 * 1024 * 1024
VMEM = pl.BlockSpec(memory_space=pltpu.VMEM)
ANY = pl.BlockSpec(memory_space=pl.ANY)


def shifted(block, distance):
    devices = lax.axis_size("seq")
    return lax.ppermute(block, "seq", [(i, (i + distance) % devices) for i in range(devices)])


def routed(block, target):
    chips = lax.axis_size("seq") // 2
    routes = [(2 * c + k, 2 * (target(c) % chips) + k) for c in range(chips) for k in range(2)]
    return lax.ppermute(block, "seq", routes)


def stop_of(c, left):
    return along(c + 4, left)


def along(c, hops):
    return c // RING * RING + (c + hops) % RING


def pack_kernel(keys, values, both, tail, part, sems):
    rows, width = keys.shape
    copies = [
        pltpu.make_async_copy(source, both.at[:, pl.ds(n * width, width)], sems.at[n])
        for n, source in enumerate((keys, values))
    ]
    for copy in copies:
        copy.start()
    for copy in copies:
        copy.wait()
    tail[...] = both[rows - tail.shape[0] :]
    part[...] = both[: part.shape[0]]


def pack(keys, values, split):
    rows, width = keys.shape
    counts = [rows, rows // 2, split]
    keys, values = (pltpu.with_memory_space_constraint(x, pltpu.HBM) for x in (keys, values))
    return pl.pallas_call(
        pack_kernel,
        out_shape=tuple(jax.ShapeDtypeStruct((n, 2 * width), keys.dtype) for n in counts),
        in_specs=[pl.BlockSpec(memory_space=pltpu.HBM)] * 2,
        out_specs=(VMEM,) * len(counts),
        scratch_shapes=[pltpu.SemaphoreType.DMA((2,))],
        compiler_params=pltpu.CompilerParams(vmem_limit_bytes=8 * 1024 * 1024),
        name="pack",
    )(keys, values)


def tiles_of(rows, kv_heads):
    return [(g, j) for g in range(kv_heads) for j in range(rows // STRIP)]


def query_tile(queries, g, j, group):
    rows = slice(j * STRIP, (j + 1) * STRIP)
    return jnp.concatenate(
        [queries[rows, (g * group + h) * HEAD : (g * group + h + 1) * HEAD] for h in range(group)],
        axis=0,
    )


def scores_of(key_rows, query):
    return lax.dot_general(
        key_rows, query, (((1,), (1,)), ((), ())), preferred_element_type=jnp.float32
    )


def summed_of(value_rows, weights):
    return lax.dot_general(
        value_rows,
        weights.astype(jnp.bfloat16),
        (((0,), (0,)), ((), ())),
        preferred_element_type=jnp.float32,
    )


def sizes_of(queries, kv_width):
    width = queries.shape[1]
    kv_heads = kv_width // HEAD
    return kv_heads, width // HEAD // kv_heads


def in_turn(tiles, ahead, finish):
    scores = ahead(0, *tiles[0])
    for t, (g, j) in enumerate(tiles):
        later = ahead(t + 1, *tiles[t + 1]) if t + 1 < len(tiles) else None
        finish(t, g, j, scores)
        scores = later


def near_kernel(queries, both, tail, acc, stats, joined):
    rows = queries.shape[0]
    kv_width = both.shape[1] // 2
    kv_heads, group = sizes_of(queries, kv_width)
    reach = tail.shape[0]
    me = lax.axis_index("seq")
    joined[:reach] = tail[...]
    joined[reach:] = both[...]
    span = reach + STRIP
    columns = group * STRIP
    key_at = lax.broadcasted_iota(jnp.int32, (span, columns), 0)
    row_at = lax.broadcasted_iota(jnp.int32, (1, columns), 1) % STRIP

    def ahead(t, g, j):
        key_rows = joined[j * STRIP : j * STRIP + span, g * HEAD : (g + 1) * HEAD]
        return scores_of(key_rows, query_tile(queries, g, j, group))

    def finish(t, g, j, scores):
        first = j * STRIP
        value_rows = joined[first : first + span, kv_width + g * HEAD : kv_width + (g + 1) * HEAD]
        least = jnp.where(me >= 1, 0, max(reach - first, 0))
        allowed = (key_at >= jnp.maximum(row_at, least)) & (key_at <= row_at + reach)
        scores = jnp.where(allowed, scores, LOW)
        top = jnp.max(scores, axis=0, keepdims=True)
        weights = jnp.exp2(scores * SCALE - top * SCALE)
        stats[t : t + 1] = top
        stats[8 + t : 9 + t] = jnp.sum(weights, axis=0, keepdims=True)
        acc[t] = summed_of(value_rows, weights)

    in_turn(tiles_of(rows, kv_heads), ahead, finish)


def add_parts(queries, pieces, acc_in, stats_in, acc, stats, flag):
    rows = queries.shape[0]
    kv_width = pieces[0][0][0].shape[1] // 2
    kv_heads, group = sizes_of(queries, kv_width)
    tiles = tiles_of(rows, kv_heads)
    me = lax.axis_index("seq")
    flag[0] = 0

    def scores_with(parts, g, j):
        query = query_tile(queries, g, j, group)
        return [scores_of(columns_of(refs, g * HEAD), query) for refs, _ in parts]

    def columns_of(refs, first):
        return jnp.concatenate([ref[:, first : first + HEAD] for ref in refs], axis=0)

    def values_of(refs, g):
        return columns_of(refs, kv_width + g * HEAD)

    def same_top(parts):
        largest = []

        def finish(t, g, j, scores):
            top = stats_in[t : t + 1]
            total = stats_in[8 + t : 9 + t]
            summed = acc_in[t]
            for part, (ref, _) in zip(scores, parts):
                weights = jnp.exp2(part * SCALE - top * SCALE)
                total = total + jnp.sum(weights, axis=0, keepdims=True)
                summed = summed + summed_of(values_of(ref, g), weights)
            stats[t : t + 1] = top
            stats[8 + t : 9 + t] = total
            acc[t] = summed
            largest.append(total)

        in_turn(tiles, lambda t, g, j: scores_with(parts, g, j), finish)
        most = jnp.max(functools.reduce(jnp.maximum, largest))
        flag[0] = jnp.where(most < MOST, 0, 1)

    def new_top():
        def one(t, g, j):
            scores = [
                jnp.where(me >= distance, part, LOW)
                for part, (_, distance) in zip(scores_with(pieces, g, j), pieces)
            ]
            old = stats_in[t : t + 1]
            top = old
            for part in scores:
                top = jnp.maximum(top, jnp.max(part, axis=0, keepdims=True))
            fade = jnp.exp2(old * SCALE - top * SCALE)
            total = stats_in[8 + t : 9 + t] * fade
            summed = acc_in[t] * fade
            for part, (ref, _) in zip(scores, pieces):
                weights = jnp.exp2(part * SCALE - top * SCALE)
                total = total + jnp.sum(weights, axis=0, keepdims=True)
                summed = summed + summed_of(values_of(ref, g), weights)
            stats[t : t + 1] = top
            stats[8 + t : 9 + t] = total
            acc[t] = summed

        for t, (g, j) in enumerate(tiles):
            one(t, g, j)

    bounds = sorted({distance for _, distance in pieces})

    @pl.when(me < bounds[0])
    def _():
        acc[...] = acc_in[...]
        stats[...] = stats_in[...]

    for low, high in zip(bounds, bounds[1:] + [None]):
        here = me >= low if high is None else (me >= low) & (me < high)

        @pl.when(here)
        def _(low=low):
            same_top([(ref, distance) for ref, distance in pieces if distance <= low])

    @pl.when(flag[0] == 1)
    def _():
        new_top()


def blocks_of(refs, distances):
    pieces = []
    for distance in dict.fromkeys(distances):
        pieces.append(([ref for ref, d in zip(refs, distances) if d == distance], distance))
    return pieces


def far_kernel(distances, queries, acc_in, stats_in, *refs):
    pieces = blocks_of(refs, distances)
    acc, stats, flag = refs[len(distances) :]
    add_parts(queries, pieces, acc_in, stats_in, acc, stats, flag)


def last_kernel(distances, queries, acc_in, stats_in, *refs):
    pieces = blocks_of(refs, distances)
    weight, out_hbm, acc, stats, flag, attended, staged, sems = refs[len(distances) :]
    rows = queries.shape[0]
    kv_heads, group = sizes_of(queries, pieces[0][0][0].shape[1] // 2)
    cuts, _, cut = staged.shape
    add_parts(queries, pieces, acc_in, stats_in, acc, stats, flag)
    for t, (g, j) in enumerate(tiles_of(rows, kv_heads)):
        done = (acc[t] / stats[8 + t : 9 + t]).astype(jnp.bfloat16)
        for h in range(group):
            head = g * group + h
            attended[j * STRIP : (j + 1) * STRIP, head * HEAD : (head + 1) * HEAD] = done[
                :, h * STRIP : (h + 1) * STRIP
            ].T

    def put(n):
        return pltpu.make_async_copy(staged.at[n], out_hbm.at[:, pl.ds(n * cut, cut)], sems.at[n])

    for n in range(cuts):
        staged[n] = jnp.dot(
            attended[...], weight[:, n * cut : (n + 1) * cut], preferred_element_type=jnp.float32
        ).astype(jnp.bfloat16)
        put(n).start()
    for n in range(cuts):
        put(n).wait()


def cost(rows, keys, width, extra=0):
    return pl.CostEstimate(
        flops=4 * rows * keys * width + extra,
        bytes_accessed=4 * rows * width * 2 + 4 * keys * 512,
        transcendentals=rows * keys * width // HEAD,
    )


def near(queries, both, tail):
    rows, width = queries.shape
    strips = rows // STRIP
    kv_heads = both.shape[1] // 2 // HEAD
    columns = width // HEAD // kv_heads * STRIP
    return pl.pallas_call(
        near_kernel,
        out_shape=(
            jax.ShapeDtypeStruct((kv_heads * strips, HEAD, columns), jnp.float32),
            jax.ShapeDtypeStruct((16, columns), jnp.float32),
        ),
        in_specs=[VMEM] * 3,
        out_specs=(VMEM, VMEM),
        scratch_shapes=[pltpu.VMEM((rows + tail.shape[0], both.shape[1]), both.dtype)],
        compiler_params=pltpu.CompilerParams(vmem_limit_bytes=LIMIT),
        cost_estimate=cost(rows, 320, width),
        name="near",
    )(queries, both, tail)


def far(queries, state, blocks, distances):
    rows, width = queries.shape
    acc, stats = state
    return pl.pallas_call(
        functools.partial(far_kernel, distances),
        out_shape=tuple(jax.ShapeDtypeStruct(x.shape, x.dtype) for x in state),
        in_specs=[VMEM] * (3 + len(blocks)),
        out_specs=(VMEM, VMEM),
        scratch_shapes=[pltpu.SMEM((1,), jnp.int32)],
        compiler_params=pltpu.CompilerParams(vmem_limit_bytes=LIMIT),
        cost_estimate=cost(rows, sum(b.shape[0] for b in blocks), width),
        name="far",
    )(queries, acc, stats, *blocks)


def last(queries, state, blocks, distances, out_weight):
    rows, width = queries.shape
    wide = out_weight.shape[1]
    cut = 512
    acc, stats = state
    return pl.pallas_call(
        functools.partial(last_kernel, distances),
        out_shape=jax.ShapeDtypeStruct((rows, wide), jnp.bfloat16),
        in_specs=[VMEM] * (4 + len(blocks)),
        out_specs=ANY,
        scratch_shapes=[
            pltpu.VMEM(acc.shape, acc.dtype),
            pltpu.VMEM(stats.shape, stats.dtype),
            pltpu.SMEM((1,), jnp.int32),
            pltpu.VMEM((rows, width), jnp.bfloat16),
            pltpu.VMEM((wide // cut, rows, cut), jnp.bfloat16),
            pltpu.SemaphoreType.DMA((wide // cut,)),
        ],
        compiler_params=pltpu.CompilerParams(vmem_limit_bytes=LIMIT),
        cost_estimate=cost(rows, sum(b.shape[0] for b in blocks), width, 2 * rows * width * wide),
        name="last",
    )(queries, acc, stats, *blocks, out_weight)


def on_device(queries, keys, values, out_weight):
    split = 256
    both, tail, part = pack(keys, values, split)
    behind = shifted(both, 2)
    part = routed(part, lambda c: stop_of(c, 3))
    before = shifted(tail, 1)
    later = shifted(both, 16)
    behind, before, part = lax.optimization_barrier((behind, before, part))
    fourth = shifted(behind, 2)
    eighth_first = routed(part, lambda c: along(c, -3))
    eighth_rest = shifted(behind[split:], 6)
    state = near(queries, both, before)
    state = far(queries, state, (behind, later), (2, 16))
    state = far(queries, state, (fourth,), (4,))
    return last(queries, state, (eighth_first, eighth_rest), (8, 8), out_weight)


def solution(mesh):
    in_specs = (P("seq", None), P("seq", None), P("seq", None), P())
    return jax.shard_map(
        on_device, mesh=mesh, in_specs=in_specs, out_specs=P("seq", None), check_vma=False
    )
```

```python
import functools
import math

import jax
import jax.numpy as jnp
from jax import lax
from jax.experimental import pallas as pl
from jax.experimental.pallas import tpu as pltpu
from jax.sharding import PartitionSpec as P

HEAD = 128
STRIP = 128
RING = 8
LOW = -1e30
MOST = 2.0**80
SCALE = math.log2(math.e) / math.sqrt(HEAD)
LIMIT = 36 * 1024 * 1024
VMEM = pl.BlockSpec(memory_space=pltpu.VMEM)
ANY = pl.BlockSpec(memory_space=pl.ANY)


def shifted(block, distance):
    devices = lax.axis_size("seq")
    return lax.ppermute(block, "seq", [(i, (i + distance) % devices) for i in range(devices)])


def routed(block, target):
    chips = lax.axis_size("seq") // 2
    routes = [(2 * c + k, 2 * (target(c) % chips) + k) for c in range(chips) for k in range(2)]
    return lax.ppermute(block, "seq", routes)


def stop_of(c, left):
    return along(c + 4, left)


def along(c, hops):
    return c // RING * RING + (c + hops) % RING


def pack_kernel(keys, values, both, tail, part, sems):
    rows, width = keys.shape
    copies = [
        pltpu.make_async_copy(source, both.at[:, pl.ds(n * width, width)], sems.at[n])
        for n, source in enumerate((keys, values))
    ]
    for copy in copies:
        copy.start()
    for copy in copies:
        copy.wait()
    tail[...] = both[rows - tail.shape[0] :]
    part[...] = both[: part.shape[0]]


def pack(keys, values, split):
    rows, width = keys.shape
    counts = [rows, rows // 2, split]
    keys, values = (pltpu.with_memory_space_constraint(x, pltpu.HBM) for x in (keys, values))
    return pl.pallas_call(
        pack_kernel,
        out_shape=tuple(jax.ShapeDtypeStruct((n, 2 * width), keys.dtype) for n in counts),
        in_specs=[pl.BlockSpec(memory_space=pltpu.HBM)] * 2,
        out_specs=(VMEM,) * len(counts),
        scratch_shapes=[pltpu.SemaphoreType.DMA((2,))],
        compiler_params=pltpu.CompilerParams(vmem_limit_bytes=8 * 1024 * 1024),
        name="pack",
    )(keys, values)


def tiles_of(rows, kv_heads):
    return [(g, j) for g in range(kv_heads) for j in range(rows // STRIP)]


def query_tile(queries, g, j, group):
    rows = slice(j * STRIP, (j + 1) * STRIP)
    return jnp.concatenate(
        [queries[rows, (g * group + h) * HEAD : (g * group + h + 1) * HEAD] for h in range(group)],
        axis=0,
    )


def scores_of(key_rows, query):
    return lax.dot_general(
        key_rows, query, (((1,), (1,)), ((), ())), preferred_element_type=jnp.float32
    )


def summed_of(value_rows, weights):
    return lax.dot_general(
        value_rows,
        weights.astype(jnp.bfloat16),
        (((0,), (0,)), ((), ())),
        preferred_element_type=jnp.float32,
    )


def sizes_of(queries, kv_width):
    width = queries.shape[1]
    kv_heads = kv_width // HEAD
    return kv_heads, width // HEAD // kv_heads


def in_turn(tiles, ahead, finish):
    scores = ahead(0, *tiles[0])
    for t, (g, j) in enumerate(tiles):
        later = ahead(t + 1, *tiles[t + 1]) if t + 1 < len(tiles) else None
        finish(t, g, j, scores)
        scores = later


def near_kernel(queries, both, tail, acc, stats, joined):
    rows = queries.shape[0]
    kv_width = both.shape[1] // 2
    kv_heads, group = sizes_of(queries, kv_width)
    reach = tail.shape[0]
    me = lax.axis_index("seq")
    joined[:reach] = tail[...]
    joined[reach:] = both[...]
    span = reach + STRIP
    columns = group * STRIP
    key_at = lax.broadcasted_iota(jnp.int32, (span, columns), 0)
    row_at = lax.broadcasted_iota(jnp.int32, (1, columns), 1) % STRIP

    def ahead(t, g, j):
        key_rows = joined[j * STRIP : j * STRIP + span, g * HEAD : (g + 1) * HEAD]
        return scores_of(key_rows, query_tile(queries, g, j, group))

    def finish(t, g, j, scores):
        first = j * STRIP
        value_rows = joined[first : first + span, kv_width + g * HEAD : kv_width + (g + 1) * HEAD]
        least = jnp.where(me >= 1, 0, max(reach - first, 0))
        allowed = (key_at >= jnp.maximum(row_at, least)) & (key_at <= row_at + reach)
        scores = jnp.where(allowed, scores, LOW)
        top = jnp.max(scores, axis=0, keepdims=True)
        weights = jnp.exp2(scores * SCALE - top * SCALE)
        stats[t : t + 1] = top
        stats[8 + t : 9 + t] = jnp.sum(weights, axis=0, keepdims=True)
        acc[t] = summed_of(value_rows, weights)

    in_turn(tiles_of(rows, kv_heads), ahead, finish)


def add_parts(queries, pieces, acc_in, stats_in, acc, stats, flag):
    rows = queries.shape[0]
    kv_width = pieces[0][0][0].shape[1] // 2
    kv_heads, group = sizes_of(queries, kv_width)
    tiles = tiles_of(rows, kv_heads)
    me = lax.axis_index("seq")
    flag[0] = 0

    def scores_with(parts, g, j):
        query = query_tile(queries, g, j, group)
        return [scores_of(columns_of(refs, g * HEAD), query) for refs, _ in parts]

    def columns_of(refs, first):
        return jnp.concatenate([ref[:, first : first + HEAD] for ref in refs], axis=0)

    def values_of(refs, g):
        return columns_of(refs, kv_width + g * HEAD)

    def same_top(parts):
        largest = []

        def finish(t, g, j, scores):
            top = stats_in[t : t + 1]
            total = stats_in[8 + t : 9 + t]
            summed = acc_in[t]
            for part, (ref, _) in zip(scores, parts):
                weights = jnp.exp2(part * SCALE - top * SCALE)
                total = total + jnp.sum(weights, axis=0, keepdims=True)
                summed = summed + summed_of(values_of(ref, g), weights)
            stats[t : t + 1] = top
            stats[8 + t : 9 + t] = total
            acc[t] = summed
            largest.append(total)

        in_turn(tiles, lambda t, g, j: scores_with(parts, g, j), finish)
        most = jnp.max(functools.reduce(jnp.maximum, largest))
        flag[0] = jnp.where(most < MOST, 0, 1)

    def new_top():
        def one(t, g, j):
            scores = [
                jnp.where(me >= distance, part, LOW)
                for part, (_, distance) in zip(scores_with(pieces, g, j), pieces)
            ]
            old = stats_in[t : t + 1]
            top = old
            for part in scores:
                top = jnp.maximum(top, jnp.max(part, axis=0, keepdims=True))
            fade = jnp.exp2(old * SCALE - top * SCALE)
            total = stats_in[8 + t : 9 + t] * fade
            summed = acc_in[t] * fade
            for part, (ref, _) in zip(scores, pieces):
                weights = jnp.exp2(part * SCALE - top * SCALE)
                total = total + jnp.sum(weights, axis=0, keepdims=True)
                summed = summed + summed_of(values_of(ref, g), weights)
            stats[t : t + 1] = top
            stats[8 + t : 9 + t] = total
            acc[t] = summed

        for t, (g, j) in enumerate(tiles):
            one(t, g, j)

    bounds = sorted({distance for _, distance in pieces})

    @pl.when(me < bounds[0])
    def _():
        acc[...] = acc_in[...]
        stats[...] = stats_in[...]

    for low, high in zip(bounds, bounds[1:] + [None]):
        here = me >= low if high is None else (me >= low) & (me < high)

        @pl.when(here)
        def _(low=low):
            same_top([(ref, distance) for ref, distance in pieces if distance <= low])

    @pl.when(flag[0] == 1)
    def _():
        new_top()


def blocks_of(refs, distances):
    pieces = []
    for distance in dict.fromkeys(distances):
        pieces.append(([ref for ref, d in zip(refs, distances) if d == distance], distance))
    return pieces


def far_kernel(distances, queries, acc_in, stats_in, *refs):
    pieces = blocks_of(refs, distances)
    acc, stats, flag = refs[len(distances) :]
    add_parts(queries, pieces, acc_in, stats_in, acc, stats, flag)


def last_kernel(distances, queries, acc_in, stats_in, *refs):
    pieces = blocks_of(refs, distances)
    weight, out_hbm, acc, stats, flag, attended, staged, sems = refs[len(distances) :]
    rows = queries.shape[0]
    kv_heads, group = sizes_of(queries, pieces[0][0][0].shape[1] // 2)
    cuts, _, cut = staged.shape
    add_parts(queries, pieces, acc_in, stats_in, acc, stats, flag)
    for t, (g, j) in enumerate(tiles_of(rows, kv_heads)):
        done = (acc[t] / stats[8 + t : 9 + t]).astype(jnp.bfloat16)
        for h in range(group):
            head = g * group + h
            attended[j * STRIP : (j + 1) * STRIP, head * HEAD : (head + 1) * HEAD] = done[
                :, h * STRIP : (h + 1) * STRIP
            ].T

    def put(n):
        return pltpu.make_async_copy(staged.at[n], out_hbm.at[:, pl.ds(n * cut, cut)], sems.at[n])

    for n in range(cuts):
        staged[n] = jnp.dot(
            attended[...], weight[:, n * cut : (n + 1) * cut], preferred_element_type=jnp.float32
        ).astype(jnp.bfloat16)
        put(n).start()
    for n in range(cuts):
        put(n).wait()


def cost(rows, keys, width, extra=0):
    return pl.CostEstimate(
        flops=4 * rows * keys * width + extra,
        bytes_accessed=4 * rows * width * 2 + 4 * keys * 512,
        transcendentals=rows * keys * width // HEAD,
    )


def near(queries, both, tail):
    rows, width = queries.shape
    strips = rows // STRIP
    kv_heads = both.shape[1] // 2 // HEAD
    columns = width // HEAD // kv_heads * STRIP
    return pl.pallas_call(
        near_kernel,
        out_shape=(
            jax.ShapeDtypeStruct((kv_heads * strips, HEAD, columns), jnp.float32),
            jax.ShapeDtypeStruct((16, columns), jnp.float32),
        ),
        in_specs=[VMEM] * 3,
        out_specs=(VMEM, VMEM),
        scratch_shapes=[pltpu.VMEM((rows + tail.shape[0], both.shape[1]), both.dtype)],
        compiler_params=pltpu.CompilerParams(vmem_limit_bytes=LIMIT),
        cost_estimate=cost(rows, 320, width),
        name="near",
    )(queries, both, tail)


def far(queries, state, blocks, distances):
    rows, width = queries.shape
    acc, stats = state
    return pl.pallas_call(
        functools.partial(far_kernel, distances),
        out_shape=tuple(jax.ShapeDtypeStruct(x.shape, x.dtype) for x in state),
        in_specs=[VMEM] * (3 + len(blocks)),
        out_specs=(VMEM, VMEM),
        scratch_shapes=[pltpu.SMEM((1,), jnp.int32)],
        compiler_params=pltpu.CompilerParams(vmem_limit_bytes=LIMIT),
        cost_estimate=cost(rows, sum(b.shape[0] for b in blocks), width),
        name="far",
    )(queries, acc, stats, *blocks)


def last(queries, state, blocks, distances, out_weight):
    rows, width = queries.shape
    wide = out_weight.shape[1]
    cut = 256
    acc, stats = state
    return pl.pallas_call(
        functools.partial(last_kernel, distances),
        out_shape=jax.ShapeDtypeStruct((rows, wide), jnp.bfloat16),
        in_specs=[VMEM] * (4 + len(blocks)),
        out_specs=ANY,
        scratch_shapes=[
            pltpu.VMEM(acc.shape, acc.dtype),
            pltpu.VMEM(stats.shape, stats.dtype),
            pltpu.SMEM((1,), jnp.int32),
            pltpu.VMEM((rows, width), jnp.bfloat16),
            pltpu.VMEM((wide // cut, rows, cut), jnp.bfloat16),
            pltpu.SemaphoreType.DMA((wide // cut,)),
        ],
        compiler_params=pltpu.CompilerParams(vmem_limit_bytes=LIMIT),
        cost_estimate=cost(rows, sum(b.shape[0] for b in blocks), width, 2 * rows * width * wide),
        name="last",
    )(queries, acc, stats, *blocks, out_weight)


def on_device(queries, keys, values, out_weight):
    split = 256
    both, tail, part = pack(keys, values, split)
    behind = shifted(both, 2)
    part = routed(part, lambda c: stop_of(c, 3))
    before = shifted(tail, 1)
    later = shifted(both, 16)
    behind, before, part = lax.optimization_barrier((behind, before, part))
    fourth = shifted(behind, 2)
    eighth_first = routed(part, lambda c: along(c, -3))
    eighth_rest = shifted(behind[split:], 6)
    state = near(queries, both, before)
    state = far(queries, state, (behind, later), (2, 16))
    state = far(queries, state, (fourth,), (4,))
    return last(queries, state, (eighth_first, eighth_rest), (8, 8), out_weight)


def solution(mesh):
    in_specs = (P("seq", None), P("seq", None), P("seq", None), P())
    return jax.shard_map(
        on_device, mesh=mesh, in_specs=in_specs, out_specs=P("seq", None), check_vma=False
    )
```
